32 devices in a mesh: dp: 1, loop: 16 (over z, y, x), head: 2 (over core).
Axes of the slice: x: 2, y: 2, z: 4, core: 2. Of those that a mesh axis runs over, the one named last changes fastest.
Arguments:
- query_embed: bfloat16 [65536, 256], P(('dp', 'loop', 'head')), may hold values from -3 to 3
- query_heads: bfloat16 [65536, 256], P(('dp', 'loop'), 'head'), may hold values from -7 to 7
- voxel_kv: bfloat16 [32768, 512], P(('dp', 'loop'), 'head'), may hold values from -7 to 7
- band_start: int32 [1024], P(('dp', 'loop')), may hold values from 0 to 255, as said below
- band_count: int32 [1024], P(('dp', 'loop')), may hold values from 2 to 4, as said below
- out_weight: bfloat16 [256, 256], replicated, may hold values from -0.375 to 0.375
- norm_gain: float32 [256], replicated, may hold values from 0.5 to 1.5
Outputs:
- refined: bfloat16 [65536, 256], P(('dp', 'loop', 'head'))
The draws below stay inside these ranges and needn't reach their ends.
Inputs may be any that keep to these rules, and one draw needn't show every extreme that they name: Query block b attends band_count[b] voxel blocks; in every draw some 64 cyclically consecutive query blocks all have the count 4, and so do the first and the last query block of every run of 64 blocks that starts at a multiple of 64. Query block b attends voxel blocks (band_start[b] + j) mod 256 for 0 <= j < band_count[b]; each of them lies at a cyclic distance of at most 3 blocks from block 16 * b // 64. For b a multiple of 64 the band starts exactly 3 blocks before that block; for b + 1 a multiple of 64 it starts exactly 1 block before that block.
All inputs are finite; a program needn't handle non-finite values.
Results may differ from the reference program's by a relative error of at most 0.008.
Values may be sent and summed in bfloat16 or wider, within the bound.
A program may use at most 64 MiB of HBM per device.

```python
import jax
import jax.numpy as jnp
from jax import lax

HEADS = 8
HEAD_DIM = 32
D = 256
QB_DEV = 64
VB_DEV = 16
MOST = 4
QUERIES = 65536
VOXELS = 32768
QBLOCKS = 1024
VBLOCKS = 256


def band_law(key):
    base_key = jax.random.fold_in(key, 101)
    count_key, run_key, jitter_key = jax.random.split(base_key, 3)
    blocks = jnp.arange(QBLOCKS, dtype=jnp.int32)
    counts = jax.random.randint(count_key, (QBLOCKS,), MOST // 2, MOST + 1, dtype=jnp.int32)
    run_start = jax.random.randint(run_key, (), 0, QBLOCKS, dtype=jnp.int32)
    in_run = jnp.mod(blocks - run_start, QBLOCKS) < QB_DEV
    position = jnp.mod(blocks, QB_DEV)
    first_here = position == 0
    last_here = position == QB_DEV - 1
    counts = jnp.where(in_run | first_here | last_here, MOST, counts).astype(jnp.int32)
    spread = max(1, VB_DEV // 32)
    jitter = jax.random.randint(jitter_key, (QBLOCKS,), -spread, spread + 1, dtype=jnp.int32)
    jitter = jnp.where(blocks == run_start, -spread, jitter)
    jitter = jnp.where(first_here, -spread, jnp.where(last_here, spread, jitter))
    diagonal = VB_DEV * blocks // QB_DEV
    starts = jnp.mod(diagonal - counts // 2 + jitter, VBLOCKS).astype(jnp.int32)
    return (starts, counts)


def draw_band_start(key, part):
    starts, counts = band_law(key)
    return starts


def draw_band_count(key, part):
    starts, counts = band_law(key)
    return counts


def draw_query_heads(key, part):
    main_key = jax.random.fold_in(key, 303)
    drawn = jnp.clip(2.5 * jax.random.normal(main_key, (QUERIES, D)), -7.0, 7.0)
    return drawn.astype(jnp.bfloat16)


def draw_voxel_kv(key, part):
    main_key = jax.random.fold_in(key, 404)
    drawn = jnp.clip(jax.random.normal(main_key, (VOXELS, 2 * D)), -7.0, 7.0)
    return drawn.astype(jnp.bfloat16)


def steps_of(rng, dims, cuts, smallest, largest):
    gain, own = 1.0, jax.random.fold_in(rng, 6)
    for dim, parts in cuts:
        draws = jnp.exp(jax.random.uniform(jax.random.fold_in(own, dim), (parts,), jnp.float32, smallest / len(cuts), largest / len(cuts)))
        gain = gain * jnp.repeat(draws, dims[dim] // parts).reshape([-1 if axis == dim else 1 for axis in range(len(dims))])
    return gain


def noise(stream_key, shape, scale, limit, cuts=(), held_as=jnp.bfloat16):
    gain = steps_of(stream_key, shape, cuts, -0.22, 0.18) if cuts else 1.0
    entries = jax.random.normal(stream_key, shape, jnp.float32) * scale * gain
    return jnp.minimum(jnp.maximum(entries, -limit), limit).astype(held_as)


def setup_inputs(seed: int = 0, part: int = 0) -> dict:
    arg_keys = jax.random.split(jax.random.key(seed), 8)
    part_splits = jax.random.split(jax.random.fold_in(arg_keys[7], part), 8)
    query_embed = noise(part_splits[0], (QUERIES, D), 0.5, 3.0, ((0, 32),))
    query_heads = draw_query_heads(jax.random.fold_in(jax.random.fold_in(arg_keys[7], part), 71), part)
    voxel_kv = draw_voxel_kv(jax.random.fold_in(jax.random.fold_in(arg_keys[7], part), 71), part)
    band_start = draw_band_start(jax.random.fold_in(jax.random.fold_in(arg_keys[7], part), 71), part)
    band_count = draw_band_count(jax.random.fold_in(jax.random.fold_in(arg_keys[7], part), 71), part)
    out_weight = noise(arg_keys[5], (D, D), D ** -0.5, 0.375)
    norm_gain = jnp.clip(1.0 + 0.1 * jax.random.normal(arg_keys[6], (D,), jnp.float32), 0.5, 1.5)
    return dict(query_embed=query_embed, query_heads=query_heads, voxel_kv=voxel_kv, band_start=band_start, band_count=band_count, out_weight=out_weight, norm_gain=norm_gain)


def reference(query_embed, query_heads, voxel_kv, band_start, band_count, out_weight, norm_gain):
    score_scale = HEAD_DIM ** (-0.5)
    kv_blocks = voxel_kv.reshape(VBLOCKS, 128, HEADS, 2, HEAD_DIM)
    query_blocks = query_heads.reshape(QBLOCKS, 64, HEADS, HEAD_DIM)
    offsets = jnp.arange(MOST, dtype=jnp.int32)

    def one_block(operands):
        queries, start, count = operands
        block_index = jnp.mod(start.astype(jnp.int32) + offsets, VBLOCKS).astype(jnp.int32)
        window = jnp.take(kv_blocks, block_index, axis=0).reshape(MOST * 128, HEADS, 2, HEAD_DIM)
        keys = window[:, :, 0, :].astype(jnp.float32)
        voxel_values = window[:, :, 1, :].astype(jnp.float32)
        scores = jnp.einsum('qhd,khd->hqk', queries.astype(jnp.float32), keys) * score_scale
        live_mask = jnp.repeat(offsets < count, 128)
        scores = jnp.where(live_mask[None, None, :], scores, -jnp.inf)
        peak = lax.optimization_barrier(jnp.max(scores, axis=2, keepdims=True))
        weights = jnp.exp(scores - peak)
        total = lax.optimization_barrier(jnp.sum(weights, axis=2))
        rounded = lax.optimization_barrier(weights.astype(jnp.bfloat16)).astype(jnp.float32)
        summed = jnp.einsum('hqk,khd->qhd', rounded, voxel_values)
        return (summed / total.T[:, :, None]).reshape(64, HEADS * HEAD_DIM)
    attended = lax.map(one_block, (query_blocks, band_start, band_count))
    attended = attended.reshape(QUERIES, D).astype(jnp.bfloat16)
    projected = jnp.dot(attended, out_weight, preferred_element_type=jnp.float32)
    mixed = query_embed.astype(jnp.float32) + projected
    centred = mixed - lax.optimization_barrier(jnp.mean(mixed, axis=1, keepdims=True))
    variance = lax.optimization_barrier(jnp.mean(centred * centred, axis=1, keepdims=True))
    refined = centred * lax.rsqrt(variance + 1e-05) * norm_gain
    return refined.astype(jnp.bfloat16)
```

```python
import functools
import math

import jax
import jax.numpy as jnp
from jax import lax
from jax.experimental import pallas as pl
from jax.experimental.pallas import tpu as pltpu
from jax.sharding import PartitionSpec as P

HEAD_DIM = 32
MOST = 4
REACH = 3
QB = 64
VB = 128
LOG_SCALE = HEAD_DIM**-0.5 * math.log2(math.e)


def prepare(kv, keys, values_t, first, count):
    lane = lax.broadcasted_iota(jnp.int32, (VB, VB), 1) // HEAD_DIM
    ones = jnp.ones((16, VB), jnp.bfloat16)

    def body(i, _):
        block = kv[pl.ds(pl.multiple_of(i * VB, VB), VB), :].astype(jnp.float32)
        low, high = block[:, :VB], block[:, VB:]
        key = jnp.where(
            lane == 0,
            low,
            jnp.where(
                lane == 1,
                pltpu.roll(low, 96, 1),
                jnp.where(lane == 2, pltpu.roll(high, 64, 1), pltpu.roll(high, 32, 1)),
            ),
        )
        value = jnp.where(
            lane == 0,
            pltpu.roll(low, 96, 1),
            jnp.where(
                lane == 1,
                pltpu.roll(low, 64, 1),
                jnp.where(lane == 2, pltpu.roll(high, 32, 1), high),
            ),
        )
        keys[pl.ds(pl.multiple_of((first + i) * VB, VB), VB), :] = key.astype(jnp.bfloat16)
        values_t[first + i, pl.ds(0, VB), :] = value.T.astype(jnp.bfloat16)
        values_t[first + i, pl.ds(VB, 16), :] = ones
        return 0

    lax.fori_loop(0, count, body, 0)


def attend_block(query, start, length, last_window, keys, values_t):
    begin = jnp.minimum(start, last_window)
    lane_head = lax.broadcasted_iota(jnp.int32, (QB, VB), 1) // HEAD_DIM
    spread = jnp.concatenate(
        [jnp.where(lane_head == h, query, jnp.zeros_like(query)) for h in range(4)], axis=0
    )
    window = keys[pl.ds(pl.multiple_of(begin * VB, VB), MOST * VB), :]
    scores = lax.dot_general(
        window, spread, (((1,), (1,)), ((), ())), preferred_element_type=jnp.float32
    )
    parts = [scores[j * VB : (j + 1) * VB] for j in range(MOST)]
    live = [
        jnp.logical_and(begin + j >= start, begin + j < start + length) for j in range(MOST)
    ]
    tops = [
        jnp.where(live[j], jnp.max(parts[j], axis=0, keepdims=True), -1e30) for j in range(MOST)
    ]
    peak = functools.reduce(jnp.maximum, tops)
    weights = jnp.concatenate(
        [
            jnp.exp2(((parts[j] - jnp.where(live[j], peak, 1e30)) * LOG_SCALE).astype(jnp.bfloat16))
            for j in range(MOST)
        ],
        axis=0,
    )
    window_t = jnp.concatenate([values_t[begin + j] for j in range(MOST)], axis=1)
    summed = jnp.dot(window_t, weights, preferred_element_type=jnp.float32)
    inverse = 1.0 / summed[VB : VB + 1, :]
    both = jnp.concatenate(
        [summed[0:64, :VB] * inverse[:, :VB], summed[64:128, VB:] * inverse[:, VB:]], axis=0
    ).T
    odd = lane_head % 2 == 1
    return jnp.where(odd, both[QB:], both[:QB]).astype(jnp.bfloat16)


def attend_kernel(starts, counts, query, left, middle, right, out, keys, values_t):
    inner = middle.shape[0] // VB
    prepare(left, keys, values_t, 0, REACH)
    prepare(middle, keys, values_t, REACH, inner)
    prepare(right, keys, values_t, REACH + inner, REACH)
    last_window = inner + 2 * REACH - MOST
    group = 4

    def body(i, _):
        for g in range(group):
            b = i * group + g
            rows = pl.ds(pl.multiple_of(b * QB, QB), QB)
            out[rows, :] = attend_block(
                query[rows, :], starts[b], counts[b], last_window, keys, values_t
            )
        return 0

    lax.fori_loop(0, query.shape[0] // QB // group, body, 0)


def local(query_embed, query_heads, voxel_kv, band_start, band_count, out_weight, norm_gain):
    loop_size = lax.axis_size("loop")
    shard_index = lax.axis_index("loop")
    vblocks = voxel_kv.shape[0] // VB
    all_vblocks = vblocks * loop_size
    halo = REACH * VB
    right = lax.ppermute(
        voxel_kv[:halo], "loop", [(s, (s - 1) % loop_size) for s in range(loop_size)]
    )
    left = lax.ppermute(
        voxel_kv[-halo:], "loop", [(s, (s + 1) % loop_size) for s in range(loop_size)]
    )
    starts = jnp.mod(band_start - shard_index * vblocks + REACH, all_vblocks)
    vmem = pl.BlockSpec(memory_space=pltpu.VMEM)
    smem = pl.BlockSpec(memory_space=pltpu.SMEM)
    attended = pl.pallas_call(
        attend_kernel,
        out_shape=jax.ShapeDtypeStruct(query_heads.shape, jnp.bfloat16),
        in_specs=[smem, smem, vmem, vmem, vmem, vmem],
        out_specs=vmem,
        scratch_shapes=[
            pltpu.VMEM(((vblocks + 2 * REACH) * VB, VB), jnp.bfloat16),
            pltpu.VMEM((vblocks + 2 * REACH, VB + 16, VB), jnp.bfloat16),
        ],
        compiler_params=pltpu.CompilerParams(vmem_limit_bytes=40 * 2**20),
    )(starts, band_count, query_heads, left, voxel_kv, right)
    row_features = lax.all_to_all(attended, "head", split_axis=0, concat_axis=1, tiled=True)
    projected = jnp.dot(row_features, out_weight, preferred_element_type=jnp.float32)
    mixed = query_embed.astype(jnp.float32) + projected
    centred = mixed - jnp.mean(mixed, axis=1, keepdims=True)
    variance = jnp.mean(centred * centred, axis=1, keepdims=True)
    refined = centred * lax.rsqrt(variance + 1e-05) * norm_gain
    return refined.astype(jnp.bfloat16)


def solution(mesh):
    placed = (
        P(("dp", "loop", "head"), None),
        P(("dp", "loop"), "head"),
        P(("dp", "loop"), "head"),
        P(("dp", "loop")),
        P(("dp", "loop")),
        P(),
        P(),
    )
    return jax.shard_map(
        local,
        mesh=mesh,
        in_specs=placed,
        out_specs=P(("dp", "loop", "head"), None),
        check_vma=False,
    )
```

```python
import functools
import math

import jax
import jax.numpy as jnp
from jax import lax
from jax.experimental import pallas as pl
from jax.experimental.pallas import tpu as pltpu
from jax.sharding import PartitionSpec as P

HEAD_DIM = 32
MOST = 4
REACH = 3
QB = 64
VB = 128
LOG_SCALE = HEAD_DIM**-0.5 * math.log2(math.e)
BF16 = jnp.bfloat16
F32 = jnp.float32


def store_values_t(block, targets):
    turned = block.T
    ones = jnp.ones((16, VB), BF16)
    for ref, index in targets:
        for h in range(4):
            ref[index + (pl.ds(h * HEAD_DIM, HEAD_DIM),)] = turned[
                (2 * h + 1) * HEAD_DIM : (2 * h + 2) * HEAD_DIM
            ]
        ref[index + (pl.ds(VB, 16),)] = ones


def scores_of(query, begin, load_window):
    lane_head = lax.broadcasted_iota(jnp.int32, (QB, VB), 1) // HEAD_DIM
    zero = jnp.zeros_like(query)
    at_0 = lane_head == 0
    at_2 = lane_head == 2
    first = [jnp.where(at_0, query, zero), jnp.where(at_2, pltpu.roll(query, 32, 1), zero)]
    second = [
        jnp.where(at_0, pltpu.roll(query, 64, 1), zero),
        jnp.where(at_2, pltpu.roll(query, 96, 1), zero),
    ]
    spread = jnp.concatenate(
        [
            jnp.concatenate(first + [zero, zero], axis=0),
            jnp.concatenate([zero, zero] + second, axis=0),
        ],
        axis=1,
    )
    return lax.dot_general(
        load_window(begin), spread, (((1,), (1,)), ((), ())), preferred_element_type=F32
    )


def finish(scores, start, begin, length, load_values):
    parts = [scores[j * VB : (j + 1) * VB] for j in range(MOST)]
    ahead = jnp.full((1, scores.shape[1]), begin - start, jnp.int32)
    many = jnp.full((1, scores.shape[1]), length, jnp.int32)
    live = [jnp.logical_and(ahead + j >= 0, ahead + j < many) for j in range(MOST)]
    tops = [
        jnp.where(live[j], jnp.max(parts[j], axis=0, keepdims=True), -1e30) for j in range(MOST)
    ]
    peak = functools.reduce(jnp.maximum, tops)
    weights = jnp.concatenate(
        [
            jnp.exp2(((parts[j] - jnp.where(live[j], peak, 1e30)) * LOG_SCALE).astype(BF16))
            for j in range(MOST)
        ],
        axis=0,
    )
    window_t = jnp.concatenate([load_values(begin + j) for j in range(MOST)], axis=1)
    summed = jnp.dot(window_t, weights, preferred_element_type=F32)
    inverse = 1.0 / summed[VB : VB + 1, :]
    both = jnp.concatenate(
        [summed[0:64, :VB] * inverse[:, :VB], summed[64:128, VB:] * inverse[:, VB:]], axis=0
    ).T
    lane_head = lax.broadcasted_iota(jnp.int32, (QB, VB), 1) // HEAD_DIM
    return jnp.where(lane_head % 2 == 1, both[QB:], both[:QB]).astype(BF16)


def attend(first, count, offset, blocks, unroll, bands, query, slots, load_window, load_values, out):
    starts, counts = bands

    def query_rows(b):
        return query[pl.ds(pl.multiple_of((first + b) * QB, QB), QB), :]

    def place(b):
        start = starts[first + b] - offset
        return start, jnp.minimum(jnp.maximum(start, 0), blocks - MOST)

    slots[0][...] = scores_of(query_rows(0), place(0)[1], load_window)

    def body(i, _):
        for g in range(2 * unroll):
            b = 2 * unroll * i + g
            after = jnp.minimum(b + 1, count - 1)
            slots[1 - g % 2][...] = scores_of(query_rows(after), place(after)[1], load_window)
            start, begin = place(b)
            out[pl.ds(pl.multiple_of(b * QB, QB), QB), :] = finish(
                slots[g % 2][...], start, begin, counts[first + b], load_values
            )
        return 0

    lax.fori_loop(0, count // (2 * unroll), body, 0)


def prepare(count, load_block, values_t):
    def body(i, _):
        store_values_t(load_block(i), [(values_t, (i,))])
        return 0

    lax.fori_loop(0, count, body, 0, unroll=True)


def rows_of(i, count, size):
    return pl.ds(pl.multiple_of(i * size, size), count * size)


def mid_kernel(starts, counts, query_hbm, kv, other, own, query, values_t, score_a, score_b, sem):
    copy = pltpu.make_async_copy(query_hbm, query, sem)
    copy.start()
    vblocks, qblocks = kv.shape[0] // VB, query.shape[0] // QB
    edge_q = qblocks // vblocks * REACH
    mid_q = qblocks // 2 - edge_q
    head = lax.axis_index("head")
    prepare(vblocks, lambda i: kv[rows_of(i, 1, VB), :], values_t)
    copy.wait()
    for side, out in ((1 - head, other), (head, own)):
        attend(
            edge_q + side * mid_q, mid_q, REACH, vblocks, 5, (starts, counts), query,
            (score_a, score_b), lambda begin: kv[rows_of(begin, MOST, VB), :],
            lambda block: values_t[block], out,
        )


def edge_kernel(
    starts, counts, query_hbm, kv_hbm, left, right, other, own,
    query, kv_edge, values_t, score_a, score_b, sems,
):
    halo, rows = left.shape[0], kv_hbm.shape[0]
    vblocks, qblocks = rows // VB, query.shape[0] // QB
    edge_q = qblocks // vblocks * REACH
    near = 2 * halo
    last = (qblocks - edge_q) * QB
    copies = [
        pltpu.make_async_copy(left, kv_edge.at[0, pl.ds(0, halo)], sems.at[0]),
        pltpu.make_async_copy(
            kv_hbm.at[pl.ds(0, near)], kv_edge.at[0, pl.ds(halo, near)], sems.at[1]
        ),
        pltpu.make_async_copy(
            kv_hbm.at[pl.ds(rows - near, near)], kv_edge.at[1, pl.ds(0, near)], sems.at[2]
        ),
        pltpu.make_async_copy(right, kv_edge.at[1, pl.ds(near, halo)], sems.at[3]),
        pltpu.make_async_copy(
            query_hbm.at[pl.ds(0, edge_q * QB)], query.at[pl.ds(0, edge_q * QB)], sems.at[4]
        ),
        pltpu.make_async_copy(
            query_hbm.at[pl.ds(last, edge_q * QB)], query.at[pl.ds(last, edge_q * QB)], sems.at[5]
        ),
    ]
    for copy in copies:
        copy.start()
    for copy in copies:
        copy.wait()
    head = lax.axis_index("head")
    for side in range(2):
        prepare(3 * REACH, lambda i: kv_edge[side, rows_of(i, 1, VB), :], values_t.at[side])
    for side, out in ((1 - head, other), (head, own)):
        attend(
            side * (qblocks - edge_q), edge_q, side * (vblocks - REACH), 3 * REACH, 3,
            (starts, counts), query, (score_a, score_b),
            lambda begin: kv_edge[side, rows_of(begin, MOST, VB), :],
            lambda block: values_t[side, block], out,
        )


def project_kernel(
    own_mid, got_mid, own_edge, got_edge, embed_hbm, weight, gain, out_hbm, embed, result, sems
):
    copy = pltpu.make_async_copy(embed_hbm, embed, sems.at[0])
    copy.start()
    head = lax.axis_index("head")
    weights = jnp.concatenate(
        [weight[rows_of(head, 1, VB), :], weight[rows_of(1 - head, 1, VB), :]], axis=0
    )
    gains = gain[...]
    tile = 256
    copy.wait()
    sends = []
    mid, edge = own_mid.shape[0], own_edge.shape[0]
    for own, got, first in (
        (own_mid, got_mid, (1 - head) * edge),
        (own_edge, got_edge, head * mid),
    ):
        for i in range(own.shape[0] // tile):
            here = slice(i * tile, (i + 1) * tile)
            there = pl.ds(pl.multiple_of(first + i * tile, tile), tile)
            features = jnp.concatenate([own[here, :], got[here, :]], axis=1)
            mixed = embed[there, :].astype(F32) + jnp.dot(
                features, weights, preferred_element_type=F32
            )
            centred = mixed - jnp.mean(mixed, axis=1, keepdims=True)
            variance = jnp.mean(centred * centred, axis=1, keepdims=True)
            result[there, :] = (centred * lax.rsqrt(variance + 1e-5) * gains).astype(BF16)
            send = pltpu.make_async_copy(
                result.at[there], out_hbm.at[there], sems.at[1 + len(sends)]
            )
            send.start()
            sends.append(send)
    for send in sends:
        send.wait()


def local(query_embed, query_heads, voxel_kv, band_start, band_count, out_weight, norm_gain):
    loop_size = lax.axis_size("loop")
    me = lax.axis_index("loop")
    vblocks, qblocks = voxel_kv.shape[0] // VB, query_heads.shape[0] // QB
    halo = REACH * VB
    edge_rows = qblocks // vblocks * REACH * QB
    mid_rows = query_heads.shape[0] // 2 - edge_rows
    vmem = pl.BlockSpec(memory_space=pltpu.VMEM)
    smem = pl.BlockSpec(memory_space=pltpu.SMEM)
    hbm = pl.BlockSpec(memory_space=pl.ANY)
    ring = range(loop_size)
    right = lax.ppermute(voxel_kv[:halo], "loop", [(s, (s - 1) % loop_size) for s in ring])
    left = lax.ppermute(voxel_kv[-halo:], "loop", [(s, (s + 1) % loop_size) for s in ring])
    starts = jnp.mod(band_start - me * vblocks + REACH, vblocks * loop_size)
    params = pltpu.CompilerParams(vmem_limit_bytes=40 * 2**20)
    query_scratch = pltpu.VMEM(query_heads.shape, BF16)
    slots = [pltpu.VMEM((MOST * VB, 4 * QB), F32)] * 2

    def cost(rows):
        return pl.CostEstimate(
            flops=rows * 2**19, bytes_accessed=rows * 2**10, transcendentals=rows * 2**11
        )

    other_mid, own_mid = pl.pallas_call(
        mid_kernel,
        out_shape=[jax.ShapeDtypeStruct((mid_rows, VB), BF16)] * 2,
        in_specs=[smem, smem, hbm, vmem],
        out_specs=[vmem, vmem],
        scratch_shapes=[
            query_scratch, pltpu.VMEM((vblocks, VB + 16, VB), BF16), *slots,
            pltpu.SemaphoreType.DMA,
        ],
        compiler_params=params,
        cost_estimate=cost(2 * mid_rows),
    )(starts, band_count, query_heads, voxel_kv)
    swap = [(0, 1), (1, 0)]
    got_mid = lax.ppermute(other_mid, "head", swap)
    other_edge, own_edge = pl.pallas_call(
        edge_kernel,
        out_shape=[jax.ShapeDtypeStruct((edge_rows, VB), BF16)] * 2,
        in_specs=[smem, smem, hbm, hbm, hbm, hbm],
        out_specs=[vmem, vmem],
        scratch_shapes=[
            query_scratch,
            pltpu.VMEM((2, 3 * halo, voxel_kv.shape[1]), BF16),
            pltpu.VMEM((2, 3 * REACH, VB + 16, VB), BF16),
            *slots,
            pltpu.SemaphoreType.DMA((6,)),
        ],
        compiler_params=params,
        cost_estimate=cost(2 * edge_rows),
    )(starts, band_count, query_heads, voxel_kv, left, right)
    got_edge = lax.ppermute(other_edge, "head", swap)
    return pl.pallas_call(
        project_kernel,
        out_shape=jax.ShapeDtypeStruct(query_embed.shape, BF16),
        in_specs=[vmem, vmem, vmem, vmem, hbm, vmem, vmem],
        out_specs=hbm,
        scratch_shapes=[
            pltpu.VMEM(query_embed.shape, BF16),
            pltpu.VMEM(query_embed.shape, BF16),
            pltpu.SemaphoreType.DMA((1 + query_embed.shape[0] // 256,)),
        ],
        compiler_params=params,
    )(own_mid, got_mid, own_edge, got_edge, query_embed, out_weight, norm_gain.reshape(1, -1))


def solution(mesh):
    placed = (
        P(("dp", "loop", "head"), None),
        P(("dp", "loop"), "head"),
        P(("dp", "loop"), "head"),
        P(("dp", "loop")),
        P(("dp", "loop")),
        P(),
        P(),
    )
    return jax.shard_map(
        local,
        mesh=mesh,
        in_specs=placed,
        out_specs=P(("dp", "loop", "head"), None),
        check_vma=False,
    )
```

```python
import functools
import math

import jax
import jax.numpy as jnp
from jax import lax
from jax.experimental import pallas as pl
from jax.experimental.pallas import tpu as pltpu
from jax.sharding import PartitionSpec as P

HEAD_DIM = 32
MOST = 4
REACH = 3
QB = 64
VB = 128
LOG_SCALE = HEAD_DIM**-0.5 * math.log2(math.e)
BF16 = jnp.bfloat16
F32 = jnp.float32


def store_values_t(block, targets):
    turned = block.T
    ones = jnp.ones((16, VB), BF16)
    for ref, index in targets:
        for h in range(4):
            ref[index + (pl.ds(h * HEAD_DIM, HEAD_DIM),)] = turned[
                (2 * h + 1) * HEAD_DIM : (2 * h + 2) * HEAD_DIM
            ]
        ref[index + (pl.ds(VB, 16),)] = ones


def scores_of(query, begin, load_window):
    lane_head = lax.broadcasted_iota(jnp.int32, (QB, VB), 1) // HEAD_DIM
    zero = jnp.zeros_like(query)
    at_0 = lane_head == 0
    at_2 = lane_head == 2
    first = [jnp.where(at_0, query, zero), jnp.where(at_2, pltpu.roll(query, 32, 1), zero)]
    second = [
        jnp.where(at_0, pltpu.roll(query, 64, 1), zero),
        jnp.where(at_2, pltpu.roll(query, 96, 1), zero),
    ]
    spread = jnp.concatenate(
        [
            jnp.concatenate(first + [zero, zero], axis=0),
            jnp.concatenate([zero, zero] + second, axis=0),
        ],
        axis=1,
    )
    return lax.dot_general(
        load_window(begin), spread, (((1,), (1,)), ((), ())), preferred_element_type=F32
    )


def finish(scores, start, begin, length, load_values):
    parts = [scores[j * VB : (j + 1) * VB] for j in range(MOST)]
    ahead = jnp.full((1, scores.shape[1]), begin - start, jnp.int32)
    many = jnp.full((1, scores.shape[1]), length, jnp.int32)
    live = [jnp.logical_and(ahead + j >= 0, ahead + j < many) for j in range(MOST)]
    tops = [
        jnp.where(live[j], jnp.max(parts[j], axis=0, keepdims=True), -1e30) for j in range(MOST)
    ]
    peak = functools.reduce(jnp.maximum, tops)
    weights = jnp.concatenate(
        [
            jnp.exp2(((parts[j] - jnp.where(live[j], peak, 1e30)) * LOG_SCALE).astype(BF16))
            for j in range(MOST)
        ],
        axis=0,
    )
    window_t = jnp.concatenate([load_values(begin + j) for j in range(MOST)], axis=1)
    summed = jnp.dot(window_t, weights, preferred_element_type=F32)
    inverse = 1.0 / summed[VB : VB + 1, :]
    both = jnp.concatenate(
        [summed[0:64, :VB] * inverse[:, :VB], summed[64:128, VB:] * inverse[:, VB:]], axis=0
    ).T
    lane_head = lax.broadcasted_iota(jnp.int32, (QB, VB), 1) // HEAD_DIM
    return jnp.where(lane_head % 2 == 1, both[QB:], both[:QB]).astype(BF16)


def attend(first, count, offset, blocks, unroll, bands, query, slots, load_window, load_values, out):
    starts, counts, vblocks, vblocks_all = bands
    home = lax.axis_index("loop") * vblocks

    def query_rows(b):
        return query[pl.ds(pl.multiple_of((first + b) * QB, QB), QB), :]

    def place(b):
        start = lax.rem(starts[first + b] - home + REACH + vblocks_all, vblocks_all) - offset
        return start, jnp.minimum(jnp.maximum(start, 0), blocks - MOST)

    slots[0][...] = scores_of(query_rows(0), place(0)[1], load_window)

    def body(i, _):
        for g in range(2 * unroll):
            b = 2 * unroll * i + g
            after = jnp.minimum(b + 1, count - 1)
            slots[1 - g % 2][...] = scores_of(query_rows(after), place(after)[1], load_window)
            start, begin = place(b)
            out[pl.ds(pl.multiple_of(b * QB, QB), QB), :] = finish(
                slots[g % 2][...], start, begin, counts[first + b], load_values
            )
        return 0

    lax.fori_loop(0, count // (2 * unroll), body, 0)


def prepare(count, load_block, values_t):
    def body(i, _):
        store_values_t(load_block(i), [(values_t, (i,))])
        return 0

    lax.fori_loop(0, count, body, 0, unroll=True)


def rows_of(i, count, size):
    return pl.ds(pl.multiple_of(i * size, size), count * size)


def load_bands(starts_hbm, counts_hbm, starts, counts, sems):
    copies = [
        pltpu.make_async_copy(starts_hbm, starts, sems.at[0]),
        pltpu.make_async_copy(counts_hbm, counts, sems.at[1]),
    ]
    for copy in copies:
        copy.start()
    return copies


def mid_attend(side, starts, counts, query, kv, values_t, slots, vblocks_all, out):
    vblocks, qblocks = kv.shape[0] // VB, query.shape[0] // QB
    edge_q = qblocks // vblocks * REACH
    mid_q = qblocks // 2 - edge_q
    attend(
        edge_q + side * mid_q, mid_q, REACH, vblocks, 5, (starts, counts, vblocks, vblocks_all),
        query, slots, lambda begin: kv[rows_of(begin, MOST, VB), :],
        lambda block: values_t[block], out,
    )


def other_mid_kernel(
    vblocks_all, starts_hbm, counts_hbm, query_hbm, kv_hbm, out, values_t,
    starts, counts, query, kv, score_a, score_b, sems,
):
    vblocks = kv.shape[0] // VB
    cuts = 4
    step = vblocks // cuts
    pieces = [
        pltpu.make_async_copy(
            kv_hbm.at[pl.ds(c * step * VB, step * VB)],
            kv.at[pl.ds(c * step * VB, step * VB)],
            sems.at[2 + c],
        )
        for c in range(cuts)
    ]
    for piece in pieces:
        piece.start()
    bands = load_bands(starts_hbm, counts_hbm, starts, counts, sems)
    copy = pltpu.make_async_copy(
        query_hbm,
        query,
        sems.at[2 + cuts],
    )
    copy.start()
    for c, piece in enumerate(pieces):
        piece.wait()
        prepare(
            step, lambda i: kv[rows_of(c * step + i, 1, VB), :],
            values_t.at[pl.ds(c * step, step)],
        )
    for band in bands:
        band.wait()
    copy.wait()
    mid_attend(
        1 - lax.axis_index("head"), starts, counts, query, kv, values_t, (score_a, score_b),
        vblocks_all, out,
    )


def own_mid_kernel(
    vblocks_all, starts_hbm, counts_hbm, query, kv, values_t, out,
    starts, counts, score_a, score_b, sems,
):
    for band in load_bands(starts_hbm, counts_hbm, starts, counts, sems):
        band.wait()
    mid_attend(
        lax.axis_index("head"), starts, counts, query, kv, values_t, (score_a, score_b),
        vblocks_all, out,
    )


def edge_kernel(
    vblocks_all, own, starts_hbm, counts_hbm, query, kv, left, right, out,
    starts, counts, kv_edge, values_t, score_a, score_b, sems,
):
    bands = load_bands(starts_hbm, counts_hbm, starts, counts, sems)
    head = lax.axis_index("head")
    side = head if own else 1 - head
    halo, rows = left.shape[0], kv.shape[0]
    vblocks, qblocks = rows // VB, query.shape[0] // QB
    edge_q = qblocks // vblocks * REACH
    near = 2 * halo

    @pl.when(side == 0)
    def _():
        kv_edge[:halo, :] = left[...]
        kv_edge[halo:, :] = kv[:near, :]

    @pl.when(side == 1)
    def _():
        kv_edge[:near, :] = kv[rows - near :, :]
        kv_edge[near:, :] = right[...]

    prepare(3 * REACH, lambda i: kv_edge[rows_of(i, 1, VB), :], values_t)
    for band in bands:
        band.wait()
    attend(
        side * (qblocks - edge_q), edge_q, side * (vblocks - REACH), 3 * REACH, 6,
        (starts, counts, vblocks, vblocks_all), query, (score_a, score_b),
        lambda begin: kv_edge[rows_of(begin, MOST, VB), :],
        lambda block: values_t[block], out,
    )


def project_kernel(
    own_mid, got_mid, own_edge, got_edge, embed_hbm, weight, gain, out_hbm, embed, result, sems
):
    copy = pltpu.make_async_copy(embed_hbm, embed, sems.at[0])
    copy.start()
    head = lax.axis_index("head")
    weights = jnp.concatenate(
        [weight[rows_of(head, 1, VB), :], weight[rows_of(1 - head, 1, VB), :]], axis=0
    )
    gains = gain[...].reshape(1, -1)
    tile = 256
    copy.wait()
    sends = []
    mid, edge = own_mid.shape[0], own_edge.shape[0]
    for own, got, first in (
        (own_mid, got_mid, (1 - head) * edge),
        (own_edge, got_edge, head * mid),
    ):
        for i in range(own.shape[0] // tile):
            here = slice(i * tile, (i + 1) * tile)
            there = pl.ds(pl.multiple_of(first + i * tile, tile), tile)
            features = jnp.concatenate([own[here, :], got[here, :]], axis=1)
            mixed = embed[there, :].astype(F32) + jnp.dot(
                features, weights, preferred_element_type=F32
            )
            centred = mixed - jnp.mean(mixed, axis=1, keepdims=True)
            variance = jnp.mean(centred * centred, axis=1, keepdims=True)
            result[there, :] = (centred * lax.rsqrt(variance + 1e-5) * gains).astype(BF16)
            send = pltpu.make_async_copy(
                result.at[there], out_hbm.at[there], sems.at[1 + len(sends)]
            )
            send.start()
            sends.append(send)
    for send in sends:
        send.wait()


def local(query_embed, query_heads, voxel_kv, band_start, band_count, out_weight, norm_gain):
    loop_size = lax.axis_size("loop")
    vblocks, qblocks = voxel_kv.shape[0] // VB, query_heads.shape[0] // QB
    halo = REACH * VB
    edge_rows = qblocks // vblocks * REACH * QB
    mid_rows = query_heads.shape[0] // 2 - edge_rows
    vmem = pl.BlockSpec(memory_space=pltpu.VMEM)
    hbm = pl.BlockSpec(memory_space=pl.ANY)
    pinned = pl.BlockSpec(memory_space=pltpu.HBM)
    ring = range(loop_size)
    vblocks_all = vblocks * loop_size
    params = pltpu.CompilerParams(vmem_limit_bytes=32 * 2**20)
    slots = [pltpu.VMEM((MOST * VB, 4 * QB), F32)] * 2
    band_scratch = [pltpu.SMEM(band_start.shape, jnp.int32)] * 2
    values_shape = (vblocks, VB + 16, VB)

    def cost(rows):
        return pl.CostEstimate(
            flops=rows * 2**19, bytes_accessed=rows * 2**10, transcendentals=rows * 2**11
        )

    other_mid, values_t = pl.pallas_call(
        functools.partial(other_mid_kernel, vblocks_all),
        out_shape=[
            jax.ShapeDtypeStruct((mid_rows, VB), BF16),
            jax.ShapeDtypeStruct(values_shape, BF16),
        ],
        in_specs=[pinned] * 4,
        out_specs=[vmem, vmem],
        scratch_shapes=[
            *band_scratch, pltpu.VMEM(query_heads.shape, BF16), pltpu.VMEM(voxel_kv.shape, BF16),
            *slots, pltpu.SemaphoreType.DMA((7,)),
        ],
        compiler_params=params,
        cost_estimate=cost(mid_rows),
    )(band_start, band_count, query_heads, voxel_kv)
    swap = [(0, 1), (1, 0)]
    first, last, other_mid = lax.optimization_barrier(
        (voxel_kv[:halo], voxel_kv[-halo:], other_mid)
    )
    right = lax.ppermute(first, "loop", [(s, (s - 1) % loop_size) for s in ring])
    left = lax.ppermute(last, "loop", [(s, (s + 1) % loop_size) for s in ring])
    got_mid = lax.ppermute(other_mid, "head", swap)
    own_mid = pl.pallas_call(
        functools.partial(own_mid_kernel, vblocks_all),
        out_shape=jax.ShapeDtypeStruct((mid_rows, VB), BF16),
        in_specs=[pinned, pinned, vmem, vmem, vmem],
        out_specs=vmem,
        scratch_shapes=[*band_scratch, *slots, pltpu.SemaphoreType.DMA((2,))],
        compiler_params=params,
        cost_estimate=cost(mid_rows),
    )(band_start, band_count, query_heads, voxel_kv, values_t)
    left, right, own_mid = lax.optimization_barrier((left, right, own_mid))

    def edge(own, left):
        return pl.pallas_call(
            functools.partial(edge_kernel, vblocks_all, own),
            out_shape=jax.ShapeDtypeStruct((edge_rows, VB), BF16),
            in_specs=[pinned, pinned, vmem, vmem, vmem, vmem],
            out_specs=vmem,
            scratch_shapes=[
                *band_scratch,
                pltpu.VMEM((3 * halo, voxel_kv.shape[1]), BF16),
                pltpu.VMEM((3 * REACH, VB + 16, VB), BF16),
                *slots,
                pltpu.SemaphoreType.DMA((2,)),
            ],
            compiler_params=params,
            cost_estimate=cost(edge_rows),
        )(band_start, band_count, query_heads, voxel_kv, left, right)

    other_edge = edge(False, left)
    other_edge, left = lax.optimization_barrier((other_edge, left))
    got_edge = lax.ppermute(other_edge, "head", swap)
    own_edge = edge(True, left)
    return pl.pallas_call(
        project_kernel,
        out_shape=jax.ShapeDtypeStruct(query_embed.shape, BF16),
        in_specs=[vmem, vmem, vmem, vmem, hbm, vmem, vmem],
        out_specs=hbm,
        scratch_shapes=[
            pltpu.VMEM(query_embed.shape, BF16),
            pltpu.VMEM(query_embed.shape, BF16),
            pltpu.SemaphoreType.DMA((1 + query_embed.shape[0] // 256,)),
        ],
        compiler_params=params,
    )(own_mid, got_mid, own_edge, got_edge, query_embed, out_weight, norm_gain)


def solution(mesh):
    placed = (
        P(("dp", "loop", "head"), None),
        P(("dp", "loop"), "head"),
        P(("dp", "loop"), "head"),
        P(("dp", "loop")),
        P(("dp", "loop")),
        P(),
        P(),
    )
    return jax.shard_map(
        local,
        mesh=mesh,
        in_specs=placed,
        out_specs=P(("dp", "loop", "head"), None),
        check_vma=False,
    )
```

```python
import functools
import math

import jax
import jax.numpy as jnp
from jax import lax
from jax.experimental import pallas as pl
from jax.experimental.pallas import tpu as pltpu
from jax.sharding import PartitionSpec as P

HEAD_DIM = 32
MOST = 4
REACH = 3
QB = 64
VB = 128
LOG_SCALE = HEAD_DIM**-0.5 * math.log2(math.e)
BF16 = jnp.bfloat16
F32 = jnp.float32


def store_values_t(block, targets):
    turned = block.T
    ones = jnp.ones((16, VB), BF16)
    for ref, index in targets:
        for h in range(4):
            ref[index + (pl.ds(h * HEAD_DIM, HEAD_DIM),)] = turned[
                (2 * h + 1) * HEAD_DIM : (2 * h + 2) * HEAD_DIM
            ]
        ref[index + (pl.ds(VB, 16),)] = ones


def scores_of(query, begin, load_window):
    lane_head = lax.broadcasted_iota(jnp.int32, (QB, VB), 1) // HEAD_DIM
    zero = jnp.zeros_like(query)
    at_0 = lane_head == 0
    at_2 = lane_head == 2
    first = [jnp.where(at_0, query, zero), jnp.where(at_2, pltpu.roll(query, 32, 1), zero)]
    second = [
        jnp.where(at_0, pltpu.roll(query, 64, 1), zero),
        jnp.where(at_2, pltpu.roll(query, 96, 1), zero),
    ]
    spread = jnp.concatenate(
        [
            jnp.concatenate(first + [zero, zero], axis=0),
            jnp.concatenate([zero, zero] + second, axis=0),
        ],
        axis=1,
    )
    return lax.dot_general(
        load_window(begin), spread, (((1,), (1,)), ((), ())), preferred_element_type=F32
    )


def finish(scores, start, begin, length, load_values):
    parts = [scores[j * VB : (j + 1) * VB] for j in range(MOST)]
    ahead = jnp.full((1, scores.shape[1]), begin - start, jnp.int32)
    many = jnp.full((1, scores.shape[1]), length, jnp.int32)
    live = [jnp.logical_and(ahead + j >= 0, ahead + j < many) for j in range(MOST)]
    tops = [
        jnp.where(live[j], jnp.max(parts[j], axis=0, keepdims=True), -1e30) for j in range(MOST)
    ]
    peak = functools.reduce(jnp.maximum, tops)
    weights = jnp.concatenate(
        [
            jnp.exp2(((parts[j] - jnp.where(live[j], peak, 1e30)) * LOG_SCALE).astype(BF16))
            for j in range(MOST)
        ],
        axis=0,
    )
    window_t = jnp.concatenate([load_values(begin + j) for j in range(MOST)], axis=1)
    summed = jnp.dot(window_t, weights, preferred_element_type=F32)
    inverse = 1.0 / summed[VB : VB + 1, :]
    both = jnp.concatenate(
        [summed[0:64, :VB] * inverse[:, :VB], summed[64:128, VB:] * inverse[:, VB:]], axis=0
    ).T
    lane_head = lax.broadcasted_iota(jnp.int32, (QB, VB), 1) // HEAD_DIM
    return jnp.where(lane_head % 2 == 1, both[QB:], both[:QB]).astype(BF16)


def attend(first, count, offset, blocks, unroll, bands, query, slots, load_window, load_values, out):
    starts, counts, vblocks, vblocks_all = bands
    home = lax.axis_index("loop") * vblocks

    def query_rows(b):
        return query[pl.ds(pl.multiple_of((first + b) * QB, QB), QB), :]

    def place(b):
        start = lax.rem(starts[first + b] - home + REACH + vblocks_all, vblocks_all) - offset
        return start, jnp.minimum(jnp.maximum(start, 0), blocks - MOST)

    slots[0][...] = scores_of(query_rows(0), place(0)[1], load_window)

    def body(i, _):
        for g in range(2 * unroll):
            b = 2 * unroll * i + g
            after = jnp.minimum(b + 1, count - 1)
            slots[1 - g % 2][...] = scores_of(query_rows(after), place(after)[1], load_window)
            start, begin = place(b)
            out[pl.ds(pl.multiple_of(b * QB, QB), QB), :] = finish(
                slots[g % 2][...], start, begin, counts[first + b], load_values
            )
        return 0

    lax.fori_loop(0, count // (2 * unroll), body, 0)


def prepare(count, load_block, values_t):
    def body(i, _):
        store_values_t(load_block(i), [(values_t, (i,))])
        return 0

    lax.fori_loop(0, count, body, 0, unroll=True)


def rows_of(i, count, size):
    return pl.ds(pl.multiple_of(i * size, size), count * size)


def load_bands(starts_hbm, counts_hbm, starts, counts, sems):
    copies = [
        pltpu.make_async_copy(starts_hbm, starts, sems.at[0]),
        pltpu.make_async_copy(counts_hbm, counts, sems.at[1]),
    ]
    for copy in copies:
        copy.start()
    return copies


def mid_attend(side, starts, counts, query, kv, values_t, slots, vblocks_all, out):
    vblocks, qblocks = kv.shape[0] // VB, query.shape[0] // QB
    edge_q = qblocks // vblocks * REACH
    mid_q = qblocks // 2 - edge_q
    attend(
        edge_q + side * mid_q, mid_q, REACH, vblocks, 10, (starts, counts, vblocks, vblocks_all),
        query, slots, lambda begin: kv[rows_of(begin, MOST, VB), :],
        lambda block: values_t[block], out,
    )


def other_mid_kernel(
    vblocks_all, starts_hbm, counts_hbm, query, kv, out, values_t,
    starts, counts, score_a, score_b, sems,
):
    copies = load_bands(starts_hbm, counts_hbm, starts, counts, sems)
    prepare(kv.shape[0] // VB, lambda i: kv[rows_of(i, 1, VB), :], values_t)
    for copy in copies:
        copy.wait()
    mid_attend(
        1 - lax.axis_index("head"), starts, counts, query, kv, values_t, (score_a, score_b),
        vblocks_all, out,
    )


def own_mid_kernel(
    vblocks_all, starts_hbm, counts_hbm, query, kv, values_t, out,
    starts, counts, score_a, score_b, sems,
):
    for band in load_bands(starts_hbm, counts_hbm, starts, counts, sems):
        band.wait()
    mid_attend(
        lax.axis_index("head"), starts, counts, query, kv, values_t, (score_a, score_b),
        vblocks_all, out,
    )


def edge_kernel(
    vblocks_all, own, starts_hbm, counts_hbm, query, kv, left, right, out,
    starts, counts, kv_edge, values_t, score_a, score_b, sems,
):
    bands = load_bands(starts_hbm, counts_hbm, starts, counts, sems)
    head = lax.axis_index("head")
    side = head if own else 1 - head
    halo, rows = left.shape[0], kv.shape[0]
    vblocks, qblocks = rows // VB, query.shape[0] // QB
    edge_q = qblocks // vblocks * REACH
    near = 2 * halo

    @pl.when(side == 0)
    def _():
        kv_edge[:halo, :] = left[...]
        kv_edge[halo:, :] = kv[:near, :]

    @pl.when(side == 1)
    def _():
        kv_edge[:near, :] = kv[rows - near :, :]
        kv_edge[near:, :] = right[...]

    prepare(3 * REACH, lambda i: kv_edge[rows_of(i, 1, VB), :], values_t)
    for band in bands:
        band.wait()
    attend(
        side * (qblocks - edge_q), edge_q, side * (vblocks - REACH), 3 * REACH, 6,
        (starts, counts, vblocks, vblocks_all), query, (score_a, score_b),
        lambda begin: kv_edge[rows_of(begin, MOST, VB), :],
        lambda block: values_t[block], out,
    )


def project_kernel(
    own_mid, got_mid, own_edge, got_edge, embed_hbm, weight, gain, out_hbm, embed, result, sems
):
    copy = pltpu.make_async_copy(embed_hbm, embed, sems.at[0])
    copy.start()
    head = lax.axis_index("head")
    weights = jnp.concatenate(
        [weight[rows_of(head, 1, VB), :], weight[rows_of(1 - head, 1, VB), :]], axis=0
    )
    gains = gain[...].reshape(1, -1)
    tile = 256
    copy.wait()
    sends = []
    mid, edge = own_mid.shape[0], own_edge.shape[0]
    for own, got, first in (
        (own_mid, got_mid, (1 - head) * edge),
        (own_edge, got_edge, head * mid),
    ):
        for i in range(own.shape[0] // tile):
            here = slice(i * tile, (i + 1) * tile)
            there = pl.ds(pl.multiple_of(first + i * tile, tile), tile)
            features = jnp.concatenate([own[here, :], got[here, :]], axis=1)
            mixed = embed[there, :].astype(F32) + jnp.dot(
                features, weights, preferred_element_type=F32
            )
            centred = mixed - jnp.mean(mixed, axis=1, keepdims=True)
            variance = jnp.mean(centred * centred, axis=1, keepdims=True)
            result[there, :] = (centred * lax.rsqrt(variance + 1e-5) * gains).astype(BF16)
            send = pltpu.make_async_copy(
                result.at[there], out_hbm.at[there], sems.at[1 + len(sends)]
            )
            send.start()
            sends.append(send)
    for send in sends:
        send.wait()


def local(query_embed, query_heads, voxel_kv, band_start, band_count, out_weight, norm_gain):
    loop_size = lax.axis_size("loop")
    vblocks, qblocks = voxel_kv.shape[0] // VB, query_heads.shape[0] // QB
    halo = REACH * VB
    edge_rows = qblocks // vblocks * REACH * QB
    mid_rows = query_heads.shape[0] // 2 - edge_rows
    vmem = pl.BlockSpec(memory_space=pltpu.VMEM)
    hbm = pl.BlockSpec(memory_space=pl.ANY)
    pinned = pl.BlockSpec(memory_space=pltpu.HBM)
    ring = range(loop_size)
    vblocks_all = vblocks * loop_size
    params = pltpu.CompilerParams(vmem_limit_bytes=32 * 2**20)
    slots = [pltpu.VMEM((MOST * VB, 4 * QB), F32)] * 2
    band_scratch = [pltpu.SMEM(band_start.shape, jnp.int32)] * 2
    values_shape = (vblocks, VB + 16, VB)

    def cost(rows):
        return pl.CostEstimate(
            flops=rows * 2**19, bytes_accessed=rows * 2**10, transcendentals=rows * 2**11
        )

    other_mid, values_t = pl.pallas_call(
        functools.partial(other_mid_kernel, vblocks_all),
        out_shape=[
            jax.ShapeDtypeStruct((mid_rows, VB), BF16),
            jax.ShapeDtypeStruct(values_shape, BF16),
        ],
        in_specs=[pinned, pinned, vmem, vmem],
        out_specs=[vmem] * 2,
        scratch_shapes=[*band_scratch, *slots, pltpu.SemaphoreType.DMA((2,))],
        compiler_params=params,
        cost_estimate=cost(mid_rows),
    )(band_start, band_count, query_heads, voxel_kv)
    swap = [(0, 1), (1, 0)]
    first, last, other_mid = lax.optimization_barrier(
        (voxel_kv[:halo], voxel_kv[-halo:], other_mid)
    )
    right = lax.ppermute(first, "loop", [(s, (s - 1) % loop_size) for s in ring])
    left = lax.ppermute(last, "loop", [(s, (s + 1) % loop_size) for s in ring])
    got_mid = lax.ppermute(other_mid, "head", swap)
    own_mid = pl.pallas_call(
        functools.partial(own_mid_kernel, vblocks_all),
        out_shape=jax.ShapeDtypeStruct((mid_rows, VB), BF16),
        in_specs=[pinned, pinned, vmem, vmem, vmem],
        out_specs=vmem,
        scratch_shapes=[*band_scratch, *slots, pltpu.SemaphoreType.DMA((2,))],
        compiler_params=params,
        cost_estimate=cost(mid_rows),
    )(band_start, band_count, query_heads, voxel_kv, values_t)
    left, right, own_mid = lax.optimization_barrier((left, right, own_mid))

    def edge(own, left):
        return pl.pallas_call(
            functools.partial(edge_kernel, vblocks_all, own),
            out_shape=jax.ShapeDtypeStruct((edge_rows, VB), BF16),
            in_specs=[pinned, pinned, vmem, vmem, vmem, vmem],
            out_specs=vmem,
            scratch_shapes=[
                *band_scratch,
                pltpu.VMEM((3 * halo, voxel_kv.shape[1]), BF16),
                pltpu.VMEM((3 * REACH, VB + 16, VB), BF16),
                *slots,
                pltpu.SemaphoreType.DMA((2,)),
            ],
            compiler_params=params,
            cost_estimate=cost(edge_rows),
        )(band_start, band_count, query_heads, voxel_kv, left, right)

    other_edge = edge(False, left)
    other_edge, left = lax.optimization_barrier((other_edge, left))
    got_edge = lax.ppermute(other_edge, "head", swap)
    own_edge = edge(True, left)
    return pl.pallas_call(
        project_kernel,
        out_shape=jax.ShapeDtypeStruct(query_embed.shape, BF16),
        in_specs=[vmem, vmem, vmem, vmem, hbm, vmem, vmem],
        out_specs=hbm,
        scratch_shapes=[
            pltpu.VMEM(query_embed.shape, BF16),
            pltpu.VMEM(query_embed.shape, BF16),
            pltpu.SemaphoreType.DMA((1 + query_embed.shape[0] // 256,)),
        ],
        compiler_params=params,
    )(own_mid, got_mid, own_edge, got_edge, query_embed, out_weight, norm_gain)


def solution(mesh):
    placed = (
        P(("dp", "loop", "head"), None),
        P(("dp", "loop"), "head"),
        P(("dp", "loop"), "head"),
        P(("dp", "loop")),
        P(("dp", "loop")),
        P(),
        P(),
    )
    return jax.shard_map(
        local,
        mesh=mesh,
        in_specs=placed,
        out_specs=P(("dp", "loop", "head"), None),
        check_vma=False,
    )
```
